512 devices in a mesh: rep: 16 (over z_lo, core), shard: 32 (over z_hi, y, x).
Axes of the slice: x: 4, y: 4, z: 16 (z_hi: 2, z_lo: 8; z = z_hi * 8 + z_lo), core: 2. Of those that a mesh axis runs over, the one named last changes fastest.
Arguments:
- layer_input: bfloat16 [65536, 8192], P(('rep', 'shard')), may hold values from -24 to 24
- queries: bfloat16 [65536, 512], P(('rep', 'shard')), may hold values from -10 to 10
- d_out: bfloat16 [65536, 512], P(('rep', 'shard')), may hold values from -6 to 6
- segment_ids: int32 [512, 128], P(('rep', 'shard')), may hold values from 0 to 3, never falling along the last dimension, each value on 1 to 64 neighbouring positions
- kv_weight: bfloat16 [8192, 256], P('shard'), may hold values from -0.0625 to 0.0625
Outputs:
- d_input: bfloat16 [65536, 8192], P(('rep', 'shard'))
- d_queries: bfloat16 [65536, 512], P(('rep', 'shard'))
- d_kv_weight: float32 [8192, 256], P('shard')
The draws below stay inside these ranges and needn't reach their ends.
All inputs are finite; a program needn't handle non-finite values.
Results may differ from the reference program's by a relative error of at most 0.03.
Values may be sent and summed in bfloat16 or wider, within the bound.
A program may use at most 64 MiB of HBM per device.

```python
import math
import jax
import jax.numpy as jnp
import numpy as np
from jax import lax

D = 8192
HEAD = 128
QH = 4
TOK_DEV = 128
GROUPS = 512
TOKENS = 65536


def draw_queries(key, part):
    key = jax.random.fold_in(key, 7)
    base = jax.random.fold_in(key, 0)
    values = jnp.clip(jax.random.normal(base, (TOKENS, QH * HEAD), jnp.float32), -6.0, 6.0)
    return values.astype(jnp.bfloat16)


def with_spikes(result, key, source, target, blocks, factor):
    owner, partner = [(jnp.arange(result.shape[dim]) // (result.shape[dim] // blocks)).reshape([-1 if axis == dim else 1 for axis in range(result.ndim)]) for dim in (source, target)]
    chosen = jax.random.permutation(key, blocks)[partner]
    strong = (owner == chosen) | (owner == (partner + blocks // 2) % blocks)
    return jnp.where(strong, factor * result, result)


def steps_of(stream_key, dims, cuts, smallest, largest):
    def one(axis_at, blocks):
        draws = jax.random.uniform(jax.random.fold_in(jax.random.fold_in(stream_key, 6), axis_at), (blocks,), jnp.float32, smallest / len(cuts), largest / len(cuts))
        return jnp.repeat(jnp.exp(draws), dims[axis_at] // blocks).reshape((-1,) + (1,) * (len(dims) - axis_at - 1))

    gain = one(*cuts[0])
    for cut in cuts[1:]:
        gain = gain * one(*cut)
    return gain


def profile(amount, total, most, slope):
    portions = [(1 << 20) // math.isqrt(grade ** slope) + 1 for grade in range(2, amount + 1)]
    surplus, counts = total - most - (amount - 1), [1] * (amount - 1)
    while surplus > 0:
        free = [i for i in range(amount - 1) if counts[i] < most]
        whole, remaining = sum([portions[i] for i in free]), surplus
        for i in free:
            more = min(most - counts[i], max(1, remaining * portions[i] // whole), surplus)
            counts[i] = counts[i] + more
            surplus = surplus - more
    return np.array([most] + counts)


def uneven_parts(key, amount, total, reach, skew):
    if amount == 2:
        one = jax.random.randint(key, (), max(1, total - reach), min(reach, total - 1) + 1)
        return jnp.stack([one, total - one])
    sizes = jnp.asarray(profile(amount, total, reach, skew), jnp.int32)
    pairs = (amount - 1) // 2
    source_of, receiver = sizes[1:1 + 2 * pairs:2], sizes[2:2 + 2 * pairs:2]
    room = jnp.minimum(source_of - 1, reach - receiver)
    passed = jax.random.randint(jax.random.fold_in(key, 1), (pairs,), 0, 1 << 20) % (room + 1)
    sizes = sizes.at[1:1 + 2 * pairs:2].set(source_of - passed).at[2:2 + 2 * pairs:2].set(receiver + passed)
    return sizes[jax.random.permutation(jax.random.fold_in(key, 2), amount)]


def normal_values(key, extent, spread, reach, pieces=(), kind=jnp.bfloat16):
    drawn = jax.random.normal(key, extent, jnp.float32) * spread
    if len(pieces) > 0:
        drawn = steps_of(key, extent, pieces, -0.22, 0.18) * drawn
    return jnp.clip(drawn, min=-reach, max=reach).astype(kind)


def noise_with(key, shape, deviation, limit, cuts, heavy, held_as=jnp.bfloat16):
    entries = deviation * jax.random.normal(key, shape, jnp.float32)
    if cuts:
        entries = entries * steps_of(key, shape, cuts, -0.22, 0.18)
    return jnp.clip(with_spikes(entries, jax.random.fold_in(key, 3), *heavy), -limit, limit).astype(held_as)


def setup_inputs(seed: int = 0) -> dict:
    seeds = jax.random.split(jax.random.key(seed), 6)
    return {
        "layer_input": noise_with(seeds[0], (TOKENS, D), 1.0, 24.0, ((0, 512),), (0, 1, 512, 6.0)),
        "queries": draw_queries(jax.random.fold_in(seeds[5], 71), 0),
        "d_out": normal_values(seeds[2], (TOKENS, QH * HEAD), 1.0, 6.0, ((0, 512),)),
        "segment_ids": jax.vmap(lambda own: jnp.searchsorted(jnp.cumsum(uneven_parts(own, 4, TOK_DEV, TOK_DEV // 2, 1)), jnp.arange(TOK_DEV), side="right"))(jax.random.split(seeds[3], GROUPS)).reshape((GROUPS, TOK_DEV)).astype(jnp.int32),
        "kv_weight": normal_values(seeds[4], (D, 2 * HEAD), D ** -0.5, 0.0625, ((0, 32),)),
    }


def attention_grad(queries, keyval, d_out, segment):
    rows = queries.shape[0]
    scale = 1.0 / HEAD ** 0.5
    heads = queries.reshape(rows, QH, HEAD).astype(jnp.float32)
    grads = d_out.reshape(rows, QH, HEAD).astype(jnp.float32)
    keys = keyval[:, :HEAD].astype(jnp.float32)
    values = keyval[:, HEAD:].astype(jnp.float32)
    position = jnp.arange(rows)
    allowed = (segment[:, None] == segment[None, :]) & (position[None, :] <= position[:, None])
    scores = jnp.einsum('thd,sd->hts', heads, keys) * scale
    scores = jnp.where(allowed[None], scores, -1e+30)
    top = lax.optimization_barrier(jnp.max(scores, axis=2, keepdims=True))
    weights = jnp.where(allowed[None], jnp.exp(scores - top), 0.0)
    probs = weights / lax.optimization_barrier(jnp.sum(weights, axis=2, keepdims=True))
    probs_low = probs.astype(jnp.bfloat16).astype(jnp.float32)
    attended = jnp.einsum('hts,sd->thd', probs_low, values)
    delta = lax.optimization_barrier(jnp.sum(grads * attended, axis=2))
    dprob = jnp.einsum('thd,sd->hts', grads, values)
    dscore = (probs * (dprob - jnp.transpose(delta)[:, :, None])).astype(jnp.bfloat16).astype(jnp.float32)
    d_queries = (jnp.einsum('hts,sd->thd', dscore, keys) * scale).astype(jnp.bfloat16)
    d_keys = jnp.einsum('hts,thd->sd', dscore, heads) * scale
    d_values = jnp.einsum('hts,thd->sd', probs_low, grads)
    d_keyval = jnp.concatenate([d_keys, d_values], axis=1).astype(jnp.bfloat16)
    return (d_queries.reshape(rows, QH * HEAD), d_keyval)

def reference(layer_input, queries, d_out, segment_ids, kv_weight):
    keyval = jnp.dot(layer_input, kv_weight, preferred_element_type=jnp.float32).astype(jnp.bfloat16)
    blocks = (queries.reshape(GROUPS, TOK_DEV, QH * HEAD), keyval.reshape(GROUPS, TOK_DEV, 2 * HEAD), d_out.reshape(GROUPS, TOK_DEV, QH * HEAD), segment_ids)
    d_queries, d_keyval = lax.map(lambda b: attention_grad(b[0], b[1], b[2], b[3]), blocks)
    d_queries = d_queries.reshape(TOKENS, QH * HEAD)
    d_keyval = d_keyval.reshape(TOKENS, 2 * HEAD)
    d_input = lax.dot_general(d_keyval, kv_weight, (((1,), (1,)), ((), ())), preferred_element_type=jnp.float32).astype(jnp.bfloat16)
    inputs3 = layer_input.reshape(GROUPS, TOK_DEV, D)
    grads3 = d_keyval.reshape(GROUPS, TOK_DEV, 2 * HEAD)

    def accumulate(total, pair):
        term = lax.dot_general(pair[0], pair[1], (((0,), (0,)), ((), ())), preferred_element_type=jnp.float32)
        low = lax.optimization_barrier(term.astype(jnp.bfloat16))
        return (total + low.astype(jnp.float32), None)
    d_kv_weight, _ = lax.scan(accumulate, jnp.zeros((D, 2 * HEAD), jnp.float32), (inputs3, grads3))
    return (d_input, d_queries, d_kv_weight)
```

```python
import jax
import jax.numpy as jnp
from jax import lax
from jax.experimental import pallas as pl
from jax.experimental.pallas import tpu as pltpu
from jax.sharding import PartitionSpec as P

HEAD = 128
QH = 4
SCALE = 1.0 / HEAD**0.5
BF16 = jnp.bfloat16
F32 = jnp.float32
MESH = pl.DeviceIdType.MESH


def dot(a, b):
    return jnp.dot(a, b, preferred_element_type=F32)


def dot_nt(a, b):
    return lax.dot_general(a, b, (((1,), (1,)), ((), ())), preferred_element_type=F32)


def dot_tn(a, b):
    return lax.dot_general(a, b, (((0,), (0,)), ((), ())), preferred_element_type=F32)


def shard_at(zh, outer, inner, core):
    y = outer * (1 - core) + inner * core
    x = inner * (1 - core) + outer * core
    return zh * 16 + y * 4 + x


def kernel(
    x_ref, q_ref, g_ref, seg_ref, w_ref,
    dx_ref, dq_ref, dw_ref,
    xb, xt, wb, qv, gv, segv, mask, part, part_in, dst, dkv, di, dqv,
    far, to_right, to_left, far_l, far_r, in_l, in_r,
    inner_out, inner_in, z_out, z_in, fin, fin_in, dwv,
    local, x_send, x_recv, w_send, w_recv, p2_send, p2_recv, m_send, m_recv,
    c_send, c_recv, dx_send, dx_recv, r1_send, r1_recv, r2_send, r2_recv,
    z_send, z_recv, f_send, f_recv,
):
    rep, shard = lax.axis_index("rep"), lax.axis_index("shard")
    core, zl = rep % 2, rep // 2
    zh, y, x = shard // 16, (shard // 4) % 4, shard % 4
    outer = y * (1 - core) + x * core
    inner = x * (1 - core) + y * core
    right, left, across = (outer + 1) % 4, (outer + 3) % 4, (outer + 2) % 4

    def on_outer(o):
        return (rep, shard_at(zh, o, inner, core))

    def on_inner(i):
        return (rep, shard_at(zh, outer, i, core))

    def on_z(half, low):
        return (low * 2 + core, shard_at(half, outer, inner, core))

    partner = (zl * 2 + 1 - core, shard)
    mirror = on_z(1 - zh, 7 - zl)

    def rows128(i):
        return pl.ds(pl.multiple_of(i * 128, 128), 128)

    def remote(src, dst_, ssem, rsem, device):
        return pltpu.make_async_remote_copy(
            src_ref=src, dst_ref=dst_, send_sem=ssem, recv_sem=rsem,
            device_id=device, device_id_type=MESH,
        )

    def arrived(ref, sem):
        pltpu.make_async_copy(ref, ref, sem).wait()

    pending = []

    def send(src, dst_, ssem, rsem, device):
        copy = remote(src, dst_, ssem, rsem, device)
        copy.start()
        pending.append(copy)

    barrier = pltpu.get_barrier_semaphore()
    friends = [partner, on_outer(right), on_outer(left)]
    friends += [on_inner((inner + d) % 4) for d in (1, 2, 3)]
    friends += [on_z(zh, (zl + d) % 8) for d in range(1, 8)]
    friends += [on_z(1 - zh, (zl + d) % 8) for d in range(8)]
    for friend in friends:
        pl.semaphore_signal(barrier, inc=1, device_id=friend, device_id_type=MESH)

    own_w = w_ref.at[rows128(core), :]
    w_here = pltpu.make_async_copy(own_w, wb.at[0, outer, rows128(inner), :], local.at[0])
    w_here.start()
    loads = [
        pltpu.make_async_copy(q_ref, qv, local.at[1]),
        pltpu.make_async_copy(g_ref, gv, local.at[2]),
        pltpu.make_async_copy(seg_ref, segv, local.at[3]),
    ]
    for load in loads:
        load.start()

    def x_columns(n, for_core):
        k, i = n // 4, n % 4
        half, o = (k // 4 + zh) % 2, k % 4
        column = shard_at(half, o, i, for_core) * 256 + for_core * 128
        return k, pl.ds(pl.multiple_of(i * 128, 128), 128), pl.ds(pl.multiple_of(column, 128), 128)

    def load_x(n, _):
        k, to, frm = x_columns(n, core)
        pltpu.make_async_copy(
            x_ref.at[:, frm], xb.at[k, pl.ds(0, 128), to], local.at[4]
        ).start()
        return 0

    lax.fori_loop(0, 32, load_x, 0)
    pl.semaphore_wait(barrier, len(friends))

    for d in (1, 3, 2):
        send(own_w, wb.at[0, outer, rows128(inner), :], w_send.at[0, d - 1], w_recv.at[0, d - 1],
             on_inner((inner + d) % 4))
    send(own_w, wb.at[1, outer, rows128(inner), :], m_send, m_recv, mirror)

    def send_x(n, _):
        k, to, frm = x_columns(n, 1 - core)
        remote(
            x_ref.at[:, frm], xb.at[k, pl.ds(128, 128), to], x_send, x_recv, partner
        ).start()
        return 0

    lax.fori_loop(0, 32, send_x, 0)

    top, bottom = pl.ds(0, 256), pl.ds(256, 256)

    def first_ring_done(h):
        for d in (1, 3, 2):
            arrived(wb.at[h, outer, rows128((inner - d + 4) % 4), :], w_recv.at[h, d - 1])

    def second_ring(h):
        def go(part_, slot, device):
            block = wb.at[h, outer, part_, :]
            send(block, block, p2_send.at[h, slot], p2_recv.at[h, slot], device)

        go(top, 0, on_outer(right))
        go(bottom, 2, on_outer(left))
        go(bottom, 1, on_outer(right))
        go(top, 3, on_outer(left))

    def relay(h):
        block = wb.at[h, left, top, :]
        arrived(block, p2_recv.at[h, 0])
        send(block, block, p2_send.at[h, 4], p2_recv.at[h, 4], on_outer(right))
        block = wb.at[h, right, bottom, :]
        arrived(block, p2_recv.at[h, 2])
        send(block, block, p2_send.at[h, 5], p2_recv.at[h, 5], on_outer(left))

    def add_block(h, o):
        part[...] += dot(xb[h * 4 + o], wb[h, o])

    def turn(h, o):
        xt[h * 4 + o] = xb[h * 4 + o].T

    w_here.wait()
    first_ring_done(0)
    second_ring(0)

    part[...] = jnp.zeros_like(part)
    for load in loads:
        load.wait()
    across_lanes = jnp.broadcast_to(segv[...], (128, 128))
    same = across_lanes.T == across_lanes
    row = lax.broadcasted_iota(jnp.int32, (128, 128), 0)
    column = lax.broadcasted_iota(jnp.int32, (128, 128), 1)
    mask[...] = jnp.where(same & (row <= column), 0.0, -1e30)

    relay(0)
    arrived(wb.at[1, outer, rows128(inner), :], m_recv)
    mirrored = wb.at[1, outer, rows128(inner), :]
    for d in (1, 3, 2):
        send(mirrored, mirrored, w_send.at[1, d - 1], w_recv.at[1, d - 1],
             on_inner((inner + d) % 4))
    arrived(xb.at[pl.ds(0, 4)], local.at[4])
    arrived(xb.at[pl.ds(0, 4)], x_recv)
    add_block(0, outer)
    first_ring_done(1)
    second_ring(1)
    for n in range(4):
        turn(0, n)
    arrived(wb.at[0, left, bottom, :], p2_recv.at[0, 1])
    add_block(0, left)
    arrived(wb.at[0, right, top, :], p2_recv.at[0, 3])
    add_block(0, right)
    relay(1)
    arrived(wb.at[0, across, top, :], p2_recv.at[0, 4])
    arrived(wb.at[0, across, bottom, :], p2_recv.at[0, 5])
    add_block(0, across)
    add_block(1, outer)
    for n in range(4):
        turn(1, n)
    arrived(wb.at[1, left, bottom, :], p2_recv.at[1, 1])
    add_block(1, left)
    arrived(wb.at[1, right, top, :], p2_recv.at[1, 3])
    add_block(1, right)
    arrived(wb.at[1, across, top, :], p2_recv.at[1, 4])
    arrived(wb.at[1, across, bottom, :], p2_recv.at[1, 5])
    add_block(1, across)

    send(part.at[pl.ds(128, 128), :], part_in, c_send.at[0], c_recv.at[0], partner)
    arrived(part_in, c_recv.at[0])
    keyval = (part[pl.ds(0, 128), :] + part_in[...]).astype(BF16)
    keys, values = keyval[:, :HEAD], keyval[:, HEAD:]

    d_keys = jnp.zeros((128, HEAD), F32)
    d_values = jnp.zeros((128, HEAD), F32)
    for n in range(QH):
        cols = pl.ds(n * HEAD, HEAD)
        q, g = qv[:, cols], gv[:, cols]
        scores = dot_nt(keys, q) * SCALE + mask[...]
        weights = jnp.exp(scores - jnp.max(scores, axis=0, keepdims=True))
        probs = weights * (1.0 / jnp.sum(weights, axis=0, keepdims=True))
        d_probs = dot_nt(values, g)
        low = probs.astype(BF16)
        delta = jnp.sum(low.astype(F32) * d_probs, axis=0, keepdims=True)
        d_score = (probs * (d_probs - delta)).astype(BF16)
        dst[:, cols] = d_score
        d_keys += dot(d_score, q)
        d_values += dot(low, g)
    dkv[pl.ds(0, 128), pl.ds(0, HEAD)] = (d_keys * SCALE).astype(BF16)
    dkv[pl.ds(0, 128), pl.ds(HEAD, HEAD)] = d_values.astype(BF16)
    send(dkv.at[pl.ds(0, 128), :], dkv.at[pl.ds(128, 128), :], c_send.at[1], c_recv.at[1], partner)

    for n in range(QH):
        cols = pl.ds(n * HEAD, HEAD)
        dqv[:, cols] = (dot_tn(dst[:, cols], keys) * SCALE).astype(BF16)
    dq_out = pltpu.make_async_copy(dqv, dq_ref, local.at[5])
    dq_out.start()
    arrived(dkv.at[pl.ds(128, 128), :], c_recv.at[1])

    def term(h, o, rows):
        return dot(xt[h * 4 + o, rows, :], dkv[...])

    def send_far(h):
        far[h, top, :] = term(h, across, top).astype(BF16)
        send(far.at[h, top, :], far_l.at[h], r1_send.at[h, 0], r1_recv.at[h, 0], on_outer(right))
        far[h, bottom, :] = term(h, across, bottom).astype(BF16)
        send(far.at[h, bottom, :], far_r.at[h], r1_send.at[h, 1], r1_recv.at[h, 1], on_outer(left))

    def send_near(h):
        to_right[h, bottom, :] = term(h, right, bottom).astype(BF16)
        send(to_right.at[h, bottom, :], in_l.at[h, bottom, :], r1_send.at[h, 2], r1_recv.at[h, 2], on_outer(right))
        to_left[h, top, :] = term(h, left, top).astype(BF16)
        send(to_left.at[h, top, :], in_r.at[h, top, :], r1_send.at[h, 3], r1_recv.at[h, 3], on_outer(left))

    def send_joined(h):
        arrived(far_l.at[h], r1_recv.at[h, 0])
        to_right[h, top, :] = (term(h, right, top) + far_l[h].astype(F32)).astype(BF16)
        send(to_right.at[h, top, :], in_l.at[h, top, :], r1_send.at[h, 4], r1_recv.at[h, 4], on_outer(right))
        arrived(far_r.at[h], r1_recv.at[h, 1])
        to_left[h, bottom, :] = (term(h, left, bottom) + far_r[h].astype(F32)).astype(BF16)
        send(to_left.at[h, bottom, :], in_r.at[h, bottom, :], r1_send.at[h, 5], r1_recv.at[h, 5], on_outer(left))

    def input_grad(h, o):
        k = h * 4 + o
        di[k] = dot_nt(dkv[...], wb[h, o]).astype(BF16)

    def store_dx(n, _):
        k, frm, to = x_columns(n, core)
        pltpu.make_async_copy(
            di.at[k, pl.ds(0, 128), frm], dx_ref.at[:, to], local.at[6]
        ).start()
        remote(
            di.at[k, pl.ds(128, 128), frm], dx_ref.at[:, to], dx_send, dx_recv, partner
        ).start()
        return 0

    send_far(0)
    send_near(0)
    send_far(1)
    send_joined(0)
    send_near(1)
    send_joined(1)
    for n in range(4):
        input_grad(0, n)
    lax.fori_loop(0, 16, store_dx, 0)

    def outer_sum(h, i):
        rows = rows128(i)
        return term(h, outer, rows) + in_l[h, rows, :].astype(F32) + in_r[h, rows, :].astype(F32)

    def inner_ring(h):
        arrived(in_l.at[h, bottom, :], r1_recv.at[h, 2])
        arrived(in_r.at[h, top, :], r1_recv.at[h, 3])
        arrived(in_l.at[h, top, :], r1_recv.at[h, 4])
        arrived(in_r.at[h, bottom, :], r1_recv.at[h, 5])
        for d in (2, 1, 3):
            i = (inner + d) % 4
            inner_out[h, d - 1] = outer_sum(h, i).astype(BF16)
            send(inner_out.at[h, d - 1], inner_in.at[h, d - 1], r2_send.at[h, d - 1],
                 r2_recv.at[h, d - 1], on_inner(i))

    def plane_sum(h):
        total = outer_sum(h, inner)
        for d in (1, 3, 2):
            arrived(inner_in.at[h, d - 1], r2_recv.at[h, d - 1])
            total += inner_in[h, d - 1].astype(F32)
        z_out[h] = total.astype(BF16)
        for d in range(8):
            if h == 0 and d == 0:
                continue
            low = (zl + d) % 8
            rows = pl.ds(pl.multiple_of(low * 16, 16), 16)
            slot = h * 8 + d
            send(z_out.at[h, rows, :], z_in.at[slot], z_send.at[slot], z_recv.at[slot],
                 on_z((zh + h) % 2, low))

    inner_ring(0)
    for n in range(4):
        input_grad(1, n)
    plane_sum(0)
    lax.fori_loop(16, 32, store_dx, 0)
    inner_ring(1)
    plane_sum(1)

    mine = pl.ds(pl.multiple_of(zl * 16, 16), 16)
    total = z_out[0, mine, :].astype(F32)
    for slot in range(1, 16):
        arrived(z_in.at[slot], z_recv.at[slot])
        total += z_in[slot].astype(F32)
    fin[mine, :] = total.astype(BF16)
    for d in range(1, 8):
        send(fin.at[mine, :], fin.at[mine, :], f_send.at[d - 1], f_recv.at[d - 1],
             on_z(zh, (zl + d) % 8))
    for d in range(1, 8):
        rows = pl.ds(pl.multiple_of(((zl - d + 8) % 8) * 16, 16), 16)
        arrived(fin.at[rows, :], f_recv.at[d - 1])
    send(fin, fin_in, c_send.at[2], c_recv.at[2], partner)
    dwv[rows128(core), :] = fin[...].astype(F32)
    arrived(fin_in, c_recv.at[2])
    dwv[rows128(1 - core), :] = fin_in[...].astype(F32)
    dw_out = pltpu.make_async_copy(dwv, dw_ref, local.at[7])
    dw_out.start()

    for copy in pending:
        copy.wait_send()
    half_x = xb.at[pl.ds(0, 4)]
    arrived(half_x, x_send)
    arrived(half_x, dx_send)
    arrived(half_x, local.at[6])
    arrived(half_x, dx_recv)
    dq_out.wait()
    dw_out.wait()


def body(layer_input, queries, d_out, segment_ids, kv_weight):
    dma = pltpu.SemaphoreType.DMA
    any_space = pl.BlockSpec(memory_space=pl.ANY)
    return pl.pallas_call(
        kernel,
        out_shape=(
            jax.ShapeDtypeStruct((128, 8192), BF16),
            jax.ShapeDtypeStruct((128, 512), BF16),
            jax.ShapeDtypeStruct((256, 256), F32),
        ),
        in_specs=[any_space] * 5,
        out_specs=(any_space,) * 3,
        scratch_shapes=[
            pltpu.VMEM((8, 256, 512), BF16),
            pltpu.VMEM((8, 512, 256), BF16),
            pltpu.VMEM((2, 4, 512, 256), BF16),
            pltpu.VMEM((128, 512), BF16),
            pltpu.VMEM((128, 512), BF16),
            pltpu.VMEM((1, 128), jnp.int32),
            pltpu.VMEM((128, 128), F32),
            pltpu.VMEM((256, 256), F32),
            pltpu.VMEM((128, 256), F32),
            pltpu.VMEM((128, 512), BF16),
            pltpu.VMEM((256, 256), BF16),
            pltpu.VMEM((8, 256, 512), BF16),
            pltpu.VMEM((128, 512), BF16),
            pltpu.VMEM((2, 512, 256), BF16),
            pltpu.VMEM((2, 512, 256), BF16),
            pltpu.VMEM((2, 512, 256), BF16),
            pltpu.VMEM((2, 256, 256), BF16),
            pltpu.VMEM((2, 256, 256), BF16),
            pltpu.VMEM((2, 512, 256), BF16),
            pltpu.VMEM((2, 512, 256), BF16),
            pltpu.VMEM((2, 3, 128, 256), BF16),
            pltpu.VMEM((2, 3, 128, 256), BF16),
            pltpu.VMEM((2, 128, 256), BF16),
            pltpu.VMEM((16, 16, 256), BF16),
            pltpu.VMEM((128, 256), BF16),
            pltpu.VMEM((128, 256), BF16),
            pltpu.VMEM((256, 256), F32),
            dma((8,)),
            dma(()),
            dma(()),
            dma((2, 3)),
            dma((2, 3)),
            dma((2, 6)),
            dma((2, 6)),
            dma(()),
            dma(()),
            dma((3,)),
            dma((3,)),
            dma(()),
            dma(()),
            dma((2, 6)),
            dma((2, 6)),
            dma((2, 3)),
            dma((2, 3)),
            dma((16,)),
            dma((16,)),
            dma((7,)),
            dma((7,)),
        ],
        compiler_params=pltpu.CompilerParams(
            collective_id=0, has_side_effects=True, vmem_limit_bytes=40 * 1024 * 1024
        ),
    )(layer_input, queries, d_out, segment_ids, kv_weight)


def solution(mesh):
    return jax.shard_map(
        body,
        mesh=mesh,
        in_specs=(
            P(("rep", "shard"), None),
            P(("rep", "shard"), None),
            P(("rep", "shard"), None),
            P(("rep", "shard"), None),
            P("shard", None),
        ),
        out_specs=(P(("rep", "shard"), None), P(("rep", "shard"), None), P("shard", None)),
        check_vma=False,
    )
```

```python
import jax
import jax.numpy as jnp
from jax import lax
from jax.experimental import pallas as pl
from jax.experimental.pallas import tpu as pltpu
from jax.sharding import PartitionSpec as P

HEAD = 128
QH = 4
SCALE = 1.0 / HEAD**0.5
BF16 = jnp.bfloat16
F32 = jnp.float32
MESH = pl.DeviceIdType.MESH


def dot(a, b):
    return jnp.dot(a, b, preferred_element_type=F32)


def dot_nt(a, b):
    return lax.dot_general(a, b, (((1,), (1,)), ((), ())), preferred_element_type=F32)


def dot_tn(a, b):
    return lax.dot_general(a, b, (((0,), (0,)), ((), ())), preferred_element_type=F32)


def shard_at(zh, outer, inner, core):
    y = outer * (1 - core) + inner * core
    x = inner * (1 - core) + outer * core
    return zh * 16 + y * 4 + x


def kernel(
    x_ref, q_ref, g_ref, seg_ref, w_ref,
    dx_ref, dq_ref, dw_ref,
    xb, xt, wb, qv, gv, segv, mask, part, part_in, dst, dkv, di, dqv,
    far, joined, far_l, far_r, in_l, in_r,
    inner_out, inner_in, z_out, z_in, fin, fin_in, dwv,
    local, x_send, x_recv, w_send, w_recv, p2_send, p2_recv, m_send, m_recv,
    c_send, c_recv, dx_send, dx_recv, r1_send, r1_recv, r2_send, r2_recv,
    z_send, z_recv, f_send, f_recv, known,
):
    rep, shard = lax.axis_index("rep"), lax.axis_index("shard")
    core, zl = rep % 2, rep // 2
    zh, y, x = shard // 16, (shard // 4) % 4, shard % 4
    outer = y * (1 - core) + x * core
    inner = x * (1 - core) + y * core
    right, left, across = (outer + 1) % 4, (outer + 3) % 4, (outer + 2) % 4

    def on_outer(o):
        return (rep, shard_at(zh, o, inner, core))

    def on_inner(i):
        return (rep, shard_at(zh, outer, i, core))

    def on_z(half, low):
        return (low * 2 + core, shard_at(half, outer, inner, core))

    partner = (zl * 2 + 1 - core, shard)
    is_edge = (zl == 0) | (zl == 7)

    def on_z_at(d):
        z = (zh * 8 + zl + d + 16) % 16
        return on_z(z // 8, z % 8)


    def rows128(i):
        return pl.ds(pl.multiple_of(i * 128, 128), 128)

    def remote(src, dst_, ssem, rsem, device):
        return pltpu.make_async_remote_copy(
            src_ref=src, dst_ref=dst_, send_sem=ssem, recv_sem=rsem,
            device_id=device, device_id_type=MESH,
        )

    started = {}

    def sem_of(name):
        return name[0].at[name[1:]] if len(name) > 1 else name[0]

    def key_of(name):
        return (id(name[0]),) + name[1:]

    def finish():
        for ref, sem in list(started.values()):
            if callable(ref):
                ref()
                del started[key_of(sem)]
            else:
                arrived(ref, sem)

    def opened(ref, sem):
        started[key_of(sem)] = (ref, sem)

    def arrived(ref, sem):
        del started[key_of(sem)]
        pltpu.make_async_copy(ref, ref, sem_of(sem)).wait()

    def send(src, dst_, ssem, rsem, device):
        remote(src, dst_, sem_of(ssem), sem_of(rsem), device).start()
        opened(src, ssem)
        opened(dst_, rsem)

    def copy_here(src, dst_, sem):
        pltpu.make_async_copy(src, dst_, sem_of(sem)).start()
        opened(dst_, sem)

    barrier = pltpu.get_barrier_semaphore()
    friends = [partner, on_outer(right), on_outer(left)]
    friends += [on_inner((inner + d) % 4) for d in (1, 2, 3)]
    friends += [on_z_at(1), on_z_at(-1)]
    near = len(friends)
    friends.append(on_z(1 - zh, 7 * (1 - zl // 4)))
    for friend in friends:
        pl.semaphore_signal(barrier, inc=1, device_id=friend, device_id_type=MESH)

    own_w = w_ref.at[rows128(core), :]
    first_w = wb.at[0, outer, rows128(inner), :]
    copy_here(own_w, first_w, (local, 0))
    copy_here(q_ref, qv, (local, 1))
    copy_here(g_ref, gv, (local, 2))
    copy_here(seg_ref, segv, (local, 3))

    def x_columns(n, for_core):
        k, i = n // 4, n % 4
        half, o = (k // 4 + zh) % 2, k % 4
        column = shard_at(half, o, i, for_core) * 256 + for_core * 128
        return k, pl.ds(pl.multiple_of(i * 128, 128), 128), pl.ds(pl.multiple_of(column, 128), 128)

    def load_x(n, _):
        k, to, frm = x_columns(n, core)
        pltpu.make_async_copy(
            x_ref.at[:, frm], xb.at[k, pl.ds(0, 128), to], local.at[4]
        ).start()
        return 0

    half_x = xb.at[pl.ds(0, 4)]
    lax.fori_loop(0, 32, load_x, 0)
    opened(half_x, (local, 4))
    pl.semaphore_wait(barrier, near + 4 * is_edge.astype(jnp.int32))

    def tell(n):
        for d in (1 << n, -(1 << n)):
            pl.semaphore_signal(known.at[n], inc=1, device_id=on_z_at(d), device_id_type=MESH)

    def heard(n):
        pl.semaphore_wait(known.at[n], 2)


    def border(n):
        edge = zl // 7
        low = (3 - n) * edge + (4 + n) * (1 - edge)
        return remote(own_w, wb.at[1, outer, rows128(inner), :], m_send.at[n], m_recv, on_z(1 - zh, low))

    @pl.when(is_edge)
    def _():
        for n in range(4):
            border(n).start()

    def border_sent():
        @pl.when(is_edge)
        def _():
            for n in range(4):
                border(n).wait_send()

    opened(border_sent, (m_send,))
    opened(first_w, (m_recv,))

    def piece(h, o, d):
        return wb.at[h, o, rows128((inner - d + 4) % 4), :]

    def spread_inner(h, src):
        for d in (2, 1, 3):
            send(src, piece(h, outer, 0), (w_send, h, d - 1), (w_recv, h, d - 1), on_inner((inner + d) % 4))

    def spread_outer(h, d, src):
        to = piece(h, outer, d)
        send(src, to, (p2_send, h, d, 0), (p2_recv, h, d, 0), on_outer(right))
        send(src, to, (p2_send, h, d, 1), (p2_recv, h, d, 1), on_outer(left))

    def pass_on(h, d):
        arrived(piece(h, outer, d), (w_recv, h, d - 1))
        spread_outer(h, d, piece(h, outer, d))

    def relay(h, d):
        first = ((inner - d + 4) % 4) * 128
        arrived(piece(h, left, d), (p2_recv, h, d, 0))
        half = wb.at[h, left, pl.ds(pl.multiple_of(first, 128), 64), :]
        send(half, half, (p2_send, h, d, 2), (p2_recv, h, d, 2), on_outer(right))
        arrived(piece(h, right, d), (p2_recv, h, d, 1))
        half = wb.at[h, right, pl.ds(pl.multiple_of(first + 64, 64), 64), :]
        send(half, half, (p2_send, h, d, 3), (p2_recv, h, d, 3), on_outer(left))

    def relayed(h, d):
        first = ((inner - d + 4) % 4) * 128
        arrived(wb.at[h, across, pl.ds(pl.multiple_of(first, 128), 64), :], (p2_recv, h, d, 2))
        arrived(wb.at[h, across, pl.ds(pl.multiple_of(first + 64, 64), 64), :], (p2_recv, h, d, 3))

    spread_inner(0, own_w)
    spread_outer(0, 0, own_w)
    tell(0)

    def send_x(n, _):
        k, to, frm = x_columns(n, 1 - core)
        remote(
            x_ref.at[:, frm], xb.at[k, pl.ds(128, 128), to], x_send, x_recv, partner
        ).start()
        return 0

    lax.fori_loop(0, 32, send_x, 0)
    opened(half_x, (x_send,))
    opened(half_x, (x_recv,))

    def add_block(h, o):
        part[...] += dot(xb[h * 4 + o], wb[h, o])

    def turn(h, o):
        xt[h * 4 + o] = xb[h * 4 + o].T

    part[...] = jnp.zeros_like(part)
    arrived(qv, (local, 1))
    arrived(gv, (local, 2))
    arrived(segv, (local, 3))
    across_lanes = jnp.broadcast_to(segv[...], (128, 128))
    same = across_lanes.T == across_lanes
    row = lax.broadcasted_iota(jnp.int32, (128, 128), 0)
    column = lax.broadcasted_iota(jnp.int32, (128, 128), 1)
    mask[...] = jnp.where(same & (row <= column), 0.0, -1e30)

    for d in (1, 3, 2):
        pass_on(0, d)
    heard(0)
    tell(1)
    for d in (0, 1, 3):
        relay(0, d)
    arrived(piece(1, outer, 0), (m_recv,))
    spread_inner(1, piece(1, outer, 0))
    spread_outer(1, 0, piece(1, outer, 0))
    relay(0, 2)
    heard(1)
    tell(2)
    arrived(first_w, (local, 0))
    arrived(half_x, (local, 4))
    arrived(half_x, (x_recv,))
    add_block(0, outer)
    turn(0, outer)
    for d in (1, 3, 2):
        pass_on(1, d)
    add_block(0, left)
    add_block(0, right)
    turn(0, left)
    turn(0, right)
    for d in range(4):
        relayed(0, d)
    relay(1, 0)
    add_block(0, across)
    turn(0, across)
    relay(1, 1)
    relay(1, 3)
    add_block(1, outer)
    turn(1, outer)
    relay(1, 2)
    add_block(1, left)
    add_block(1, right)
    turn(1, left)
    turn(1, right)
    turn(1, across)
    for d in range(4):
        relayed(1, d)
    add_block(1, across)

    send(part.at[pl.ds(128, 128), :], part_in, (c_send, 0), (c_recv, 0), partner)
    arrived(part_in, (c_recv, 0))
    keyval = (part[pl.ds(0, 128), :] + part_in[...]).astype(BF16)
    keys, values = keyval[:, :HEAD], keyval[:, HEAD:]

    d_keys = jnp.zeros((128, HEAD), F32)
    d_values = jnp.zeros((128, HEAD), F32)
    for n in range(QH):
        cols = pl.ds(n * HEAD, HEAD)
        q, g = qv[:, cols], gv[:, cols]
        scores = dot_nt(keys, q) * SCALE + mask[...]
        weights = jnp.exp(scores - jnp.max(scores, axis=0, keepdims=True))
        probs = weights * (1.0 / jnp.sum(weights, axis=0, keepdims=True))
        d_probs = dot_nt(values, g)
        low = probs.astype(BF16)
        delta = jnp.sum(low.astype(F32) * d_probs, axis=0, keepdims=True)
        d_score = (probs * (d_probs - delta)).astype(BF16)
        dst[:, cols] = d_score
        d_keys += dot(d_score, q)
        d_values += dot(low, g)
    dkv[pl.ds(0, 128), pl.ds(0, HEAD)] = (d_keys * SCALE).astype(BF16)
    dkv[pl.ds(0, 128), pl.ds(HEAD, HEAD)] = d_values.astype(BF16)
    send(dkv.at[pl.ds(0, 128), :], dkv.at[pl.ds(128, 128), :], (c_send, 1), (c_recv, 1), partner)

    for n in range(QH):
        cols = pl.ds(n * HEAD, HEAD)
        dqv[:, cols] = (dot_tn(dst[:, cols], keys) * SCALE).astype(BF16)
    copy_here(dqv, dq_ref, (local, 5))
    arrived(dkv.at[pl.ds(128, 128), :], (c_recv, 1))

    heard(2)

    def term(h, o, d):
        return dot(xt[h * 4 + o, rows128((inner + d) % 4), :], dkv[...])

    def send_far(h, d):
        far[h, d] = term(h, across, d).astype(BF16)
        send(far.at[h, d, pl.ds(0, 64), :], far_l.at[h, d], (r1_send, h, d, 0), (r1_recv, h, d, 0), on_outer(right))
        send(far.at[h, d, pl.ds(64, 64), :], far_r.at[h, d], (r1_send, h, d, 1), (r1_recv, h, d, 1), on_outer(left))

    def send_joined(h, d):
        to_right, to_left = term(h, right, d), term(h, left, d)
        arrived(far_l.at[h, d], (r1_recv, h, d, 0))
        joined[h, d, 0, pl.ds(0, 64), :] = (to_right[:64] + far_l[h, d].astype(F32)).astype(BF16)
        joined[h, d, 0, pl.ds(64, 64), :] = to_right[64:].astype(BF16)
        send(joined.at[h, d, 0], in_l.at[h, d], (r1_send, h, d, 2), (r1_recv, h, d, 2), on_outer(right))
        arrived(far_r.at[h, d], (r1_recv, h, d, 1))
        joined[h, d, 1, pl.ds(0, 64), :] = to_left[:64].astype(BF16)
        joined[h, d, 1, pl.ds(64, 64), :] = (to_left[64:] + far_r[h, d].astype(F32)).astype(BF16)
        send(joined.at[h, d, 1], in_r.at[h, d], (r1_send, h, d, 3), (r1_recv, h, d, 3), on_outer(left))

    def input_grad(h, o):
        k = h * 4 + o
        di[k] = dot_nt(dkv[...], wb[h, o]).astype(BF16)

    def store_dx(n, _):
        k, frm, to = x_columns(n, core)
        pltpu.make_async_copy(
            di.at[k, pl.ds(0, 128), frm], dx_ref.at[:, to], local.at[6 + n // 16]
        ).start()
        remote(
            di.at[k, pl.ds(128, 128), frm], dx_ref.at[:, to], dx_send.at[n // 16], dx_recv.at[n // 16], partner
        ).start()
        return 0

    def write_dx(h):
        lax.fori_loop(h * 16, h * 16 + 16, store_dx, 0)
        quarter = xb.at[pl.ds(0, 2)]
        for sem in ((local, 6 + h), (dx_send, h), (dx_recv, h)):
            opened(quarter, sem)

    def outer_sum(h, d):
        total = term(h, outer, d)
        arrived(in_l.at[h, d], (r1_recv, h, d, 2))
        total += in_l[h, d].astype(F32)
        arrived(in_r.at[h, d], (r1_recv, h, d, 3))
        return total + in_r[h, d].astype(F32)

    def inner_ring(h, d):
        inner_out[h, d - 1] = outer_sum(h, d).astype(BF16)
        send(inner_out.at[h, d - 1], inner_in.at[h, d - 1], (r2_send, h, d - 1),
             (r2_recv, h, d - 1), on_inner((inner + d) % 4))

    def plane_sum(h):
        total = outer_sum(h, 0)
        for d in (2, 1, 3):
            arrived(inner_in.at[h, d - 1], (r2_recv, h, d - 1))
            total += inner_in[h, d - 1].astype(F32)
        z_out[h] = total.astype(BF16)
        for d in range(8):
            if h == 0 and d == 0:
                continue
            low = (zl + d) % 8
            rows = pl.ds(pl.multiple_of(low * 16, 16), 16)
            slot = h * 8 + d
            send(z_out.at[h, rows, :], z_in.at[slot], (z_send, slot), (z_recv, slot),
                 on_z((zh + h) % 2, low))

    away = [(1, 2), (1, 1), (1, 3), (0, 2), (0, 1), (0, 3)]
    for h, d in away + [(1, 0), (0, 0)]:
        send_far(h, d)
    for h, d in away + [(1, 0), (0, 0)]:
        send_joined(h, d)
    for h, d in away:
        inner_ring(h, d)
    plane_sum(1)
    plane_sum(0)
    for n in range(8):
        input_grad(n // 4, n % 4)
        if n % 4 == 3:
            write_dx(n // 4)

    mine = pl.ds(pl.multiple_of(zl * 16, 16), 16)
    total = z_out[0, mine, :].astype(F32)
    for slot in range(1, 16):
        arrived(z_in.at[slot], (z_recv, slot))
        total += z_in[slot].astype(F32)
    fin[mine, :] = total.astype(BF16)
    for d in range(1, 8):
        send(fin.at[mine, :], fin.at[mine, :], (f_send, d - 1), (f_recv, d - 1),
             on_z(zh, (zl + d) % 8))
    for d in range(1, 8):
        rows = pl.ds(pl.multiple_of(((zl - d + 8) % 8) * 16, 16), 16)
        arrived(fin.at[rows, :], (f_recv, d - 1))
    send(fin, fin_in, (c_send, 2), (c_recv, 2), partner)
    dwv[rows128(core), :] = fin[...].astype(F32)
    arrived(fin_in, (c_recv, 2))
    dwv[rows128(1 - core), :] = fin_in[...].astype(F32)
    copy_here(dwv, dw_ref, (local, 8))

    finish()


def store_kernel(a, b, c, a_out, b_out, c_out, sems):
    copies = [
        pltpu.make_async_copy(src, to, sems.at[n])
        for n, (src, to) in enumerate(((a, a_out), (b, b_out), (c, c_out)))
    ]
    for copy in copies:
        copy.start()
    for copy in copies:
        copy.wait()


def body(layer_input, queries, d_out, segment_ids, kv_weight):
    dma = pltpu.SemaphoreType.DMA
    any_space = pl.BlockSpec(memory_space=pl.ANY)
    shapes = (
        jax.ShapeDtypeStruct((128, 8192), BF16),
        jax.ShapeDtypeStruct((128, 512), BF16),
        jax.ShapeDtypeStruct((256, 256), F32),
    )
    results = pl.pallas_call(
        kernel,
        out_shape=shapes,
        in_specs=[pl.BlockSpec(memory_space=pltpu.HBM)] * 5,
        out_specs=(any_space,) * 3,
        scratch_shapes=[
            pltpu.VMEM((8, 256, 512), BF16),
            pltpu.VMEM((8, 512, 256), BF16),
            pltpu.VMEM((2, 4, 512, 256), BF16),
            pltpu.VMEM((128, 512), BF16),
            pltpu.VMEM((128, 512), BF16),
            pltpu.VMEM((1, 128), jnp.int32),
            pltpu.VMEM((128, 128), F32),
            pltpu.VMEM((256, 256), F32),
            pltpu.VMEM((128, 256), F32),
            pltpu.VMEM((128, 512), BF16),
            pltpu.VMEM((256, 256), BF16),
            pltpu.VMEM((8, 256, 512), BF16),
            pltpu.VMEM((128, 512), BF16),
            pltpu.VMEM((2, 4, 128, 256), BF16),
            pltpu.VMEM((2, 4, 2, 128, 256), BF16),
            pltpu.VMEM((2, 4, 64, 256), BF16),
            pltpu.VMEM((2, 4, 64, 256), BF16),
            pltpu.VMEM((2, 4, 128, 256), BF16),
            pltpu.VMEM((2, 4, 128, 256), BF16),
            pltpu.VMEM((2, 3, 128, 256), BF16),
            pltpu.VMEM((2, 3, 128, 256), BF16),
            pltpu.VMEM((2, 128, 256), BF16),
            pltpu.VMEM((16, 16, 256), BF16),
            pltpu.VMEM((128, 256), BF16),
            pltpu.VMEM((128, 256), BF16),
            pltpu.VMEM((256, 256), F32),
            dma((9,)),
            dma(()),
            dma(()),
            dma((2, 3)),
            dma((2, 3)),
            dma((2, 4, 4)),
            dma((2, 4, 4)),
            dma((4,)),
            dma(()),
            dma((3,)),
            dma((3,)),
            dma((2,)),
            dma((2,)),
            dma((2, 4, 4)),
            dma((2, 4, 4)),
            dma((2, 3)),
            dma((2, 3)),
            dma((16,)),
            dma((16,)),
            dma((7,)),
            dma((7,)),
            pltpu.SemaphoreType.REGULAR((3,)),
        ],
        compiler_params=pltpu.CompilerParams(
            collective_id=0, has_side_effects=True, vmem_limit_bytes=40 * 1024 * 1024
        ),
    )(*[
        pltpu.with_memory_space_constraint(a, pltpu.HBM)
        for a in (layer_input, queries, d_out, segment_ids, kv_weight)
    ])
    return pl.pallas_call(
        store_kernel,
        out_shape=shapes,
        in_specs=[any_space] * 3,
        out_specs=(any_space,) * 3,
        scratch_shapes=[dma((3,))],
        compiler_params=pltpu.CompilerParams(vmem_limit_bytes=4 * 1024 * 1024),
    )(*results)


def solution(mesh):
    return jax.shard_map(
        body,
        mesh=mesh,
        in_specs=(
            P(("rep", "shard"), None),
            P(("rep", "shard"), None),
            P(("rep", "shard"), None),
            P(("rep", "shard"), None),
            P("shard", None),
        ),
        out_specs=(P(("rep", "shard"), None), P(("rep", "shard"), None), P("shard", None)),
        check_vma=False,
    )
```

```python
import jax
import jax.numpy as jnp
from jax import lax
from jax.experimental import pallas as pl
from jax.experimental.pallas import tpu as pltpu
from jax.sharding import PartitionSpec as P

HEAD = 128
QH = 4
SCALE = 1.0 / HEAD**0.5
BF16 = jnp.bfloat16
F32 = jnp.float32
MESH = pl.DeviceIdType.MESH


def dot(a, b):
    return jnp.dot(a, b, preferred_element_type=F32)


def dot_nt(a, b):
    return lax.dot_general(a, b, (((1,), (1,)), ((), ())), preferred_element_type=F32)


def dot_tn(a, b):
    return lax.dot_general(a, b, (((0,), (0,)), ((), ())), preferred_element_type=F32)


def shard_at(zh, outer, inner, core):
    y = outer * (1 - core) + inner * core
    x = inner * (1 - core) + outer * core
    return zh * 16 + y * 4 + x


def kernel(
    x_ref, q_ref, g_ref, seg_ref, w_ref,
    dx_ref, dq_ref, dw_ref,
    xb, wb, qv, gv, segv, mask, part, part_in, dst, dkv, di,
    far, joined, far_l, far_r, in_l, in_r,
    inner_out, inner_in, z_out, z_in, fin,
    local, x_send, x_recv, w_send, w_recv, p2_send, p2_recv, m_send, m_recv,
    c_send, c_recv, dx_send, dx_recv, r1_send, r1_recv, r2_send, r2_recv,
    z_send, z_recv, f_send, f_recv, known,
):
    rep, shard = lax.axis_index("rep"), lax.axis_index("shard")
    core, zl = rep % 2, rep // 2
    zh, y, x = shard // 16, (shard // 4) % 4, shard % 4
    z = zh * 8 + zl
    outer = y * (1 - core) + x * core
    inner = x * (1 - core) + y * core
    right, left, across = (outer + 1) % 4, (outer + 3) % 4, (outer + 2) % 4

    def on_outer(o):
        return (rep, shard_at(zh, o, inner, core))

    def on_inner(i):
        return (rep, shard_at(zh, outer, i, core))

    def on_z(half, low):
        return (low * 2 + core, shard_at(half, outer, inner, core))

    partner = (zl * 2 + 1 - core, shard)
    is_edge = (zl == 0) | (zl == 7)

    def on_z_at(d):
        there = (z + d + 16) % 16
        return on_z(there // 8, there % 8)


    def rows128(i):
        return pl.ds(pl.multiple_of(i * 128, 128), 128)

    def remote(src, dst_, ssem, rsem, device):
        return pltpu.make_async_remote_copy(
            src_ref=src, dst_ref=dst_, send_sem=ssem, recv_sem=rsem,
            device_id=device, device_id_type=MESH,
        )

    started = {}

    def sem_of(name):
        return name[0].at[name[1:]] if len(name) > 1 else name[0]

    def key_of(name):
        return (id(name[0]),) + name[1:]

    def finish():
        for ref, sem in list(started.values()):
            if callable(ref):
                ref()
                del started[key_of(sem)]
            else:
                arrived(ref, sem)

    def opened(ref, sem):
        started[key_of(sem)] = (ref, sem)

    def arrived(ref, sem):
        del started[key_of(sem)]
        pltpu.make_async_copy(ref, ref, sem_of(sem)).wait()

    def send(src, dst_, ssem, rsem, device):
        remote(src, dst_, sem_of(ssem), sem_of(rsem), device).start()
        opened(src, ssem)
        opened(dst_, rsem)

    def copy_here(src, dst_, sem):
        pltpu.make_async_copy(src, dst_, sem_of(sem)).start()
        opened(dst_, sem)

    barrier = pltpu.get_barrier_semaphore()
    friends = [partner, on_outer(right), on_outer(left)]
    friends += [on_inner((inner + d) % 4) for d in (1, 2, 3)]
    friends += [on_z_at(1), on_z_at(-1)]
    near = len(friends)
    friends.append(on_z(1 - zh, 7 * (1 - zl // 4)))
    for friend in friends:
        pl.semaphore_signal(barrier, inc=1, device_id=friend, device_id_type=MESH)

    own_w = w_ref.at[rows128(core), :]
    first_w = wb.at[0, outer, rows128(inner), :]
    copy_here(own_w, first_w, (local, 0))
    copy_here(q_ref, qv, (local, 1))
    copy_here(g_ref, gv, (local, 2))
    copy_here(seg_ref, segv, (local, 3))

    def x_columns(n, for_core):
        k, i = n // 4, n % 4
        half, o = (k // 4 + zh) % 2, k % 4
        column = shard_at(half, o, i, for_core) * 256 + for_core * 128
        return k, pl.ds(pl.multiple_of(i * 128, 128), 128), pl.ds(pl.multiple_of(column, 128), 128)

    def load_x(n, _):
        k, to, frm = x_columns(n, core)
        pltpu.make_async_copy(
            x_ref.at[:, frm], xb.at[k, pl.ds(0, 128), to], local.at[4]
        ).start()
        return 0

    half_x = xb.at[pl.ds(0, 4)]
    pl.semaphore_wait(barrier, near + 4 * is_edge.astype(jnp.int32))

    def tell(n):
        for d in (1 << n, -(1 << n)):
            pl.semaphore_signal(known.at[n], inc=1, device_id=on_z_at(d), device_id_type=MESH)

    def heard(n):
        pl.semaphore_wait(known.at[n], 2)


    def border(n):
        edge = zl // 7
        low = (3 - n) * edge + (4 + n) * (1 - edge)
        return remote(own_w, wb.at[1, outer, rows128(inner), :], m_send.at[n], m_recv, on_z(1 - zh, low))

    @pl.when(is_edge)
    def _():
        for n in range(4):
            border(n).start()

    def border_sent():
        @pl.when(is_edge)
        def _():
            for n in range(4):
                border(n).wait_send()

    opened(border_sent, (m_send,))
    opened(first_w, (m_recv,))

    def piece(h, o, d):
        return wb.at[h, o, rows128((inner - d + 4) % 4), :]

    def spread_inner(h, src):
        for d in (2, 1, 3):
            send(src, piece(h, outer, 0), (w_send, h, d - 1), (w_recv, h, d - 1), on_inner((inner + d) % 4))

    def spread_outer(h, d, src):
        to = piece(h, outer, d)
        send(src, to, (p2_send, h, d, 0), (p2_recv, h, d, 0), on_outer(right))
        send(src, to, (p2_send, h, d, 1), (p2_recv, h, d, 1), on_outer(left))

    def pass_on(h, d):
        arrived(piece(h, outer, d), (w_recv, h, d - 1))
        spread_outer(h, d, piece(h, outer, d))

    def relay(h, d):
        first = ((inner - d + 4) % 4) * 128
        arrived(piece(h, left, d), (p2_recv, h, d, 0))
        half = wb.at[h, left, pl.ds(pl.multiple_of(first, 128), 64), :]
        send(half, half, (p2_send, h, d, 2), (p2_recv, h, d, 2), on_outer(right))
        arrived(piece(h, right, d), (p2_recv, h, d, 1))
        half = wb.at[h, right, pl.ds(pl.multiple_of(first + 64, 64), 64), :]
        send(half, half, (p2_send, h, d, 3), (p2_recv, h, d, 3), on_outer(left))

    def relayed(h, d):
        first = ((inner - d + 4) % 4) * 128
        arrived(wb.at[h, across, pl.ds(pl.multiple_of(first, 128), 64), :], (p2_recv, h, d, 2))
        arrived(wb.at[h, across, pl.ds(pl.multiple_of(first + 64, 64), 64), :], (p2_recv, h, d, 3))

    spread_inner(0, own_w)
    spread_outer(0, 0, own_w)
    tell(0)

    def send_x(n, _):
        k, to, frm = x_columns(n, 1 - core)
        remote(
            x_ref.at[:, frm], xb.at[k, pl.ds(128, 128), to], x_send, x_recv, partner
        ).start()
        return 0

    lax.fori_loop(0, 32, load_x, 0)
    opened(half_x, (local, 4))
    lax.fori_loop(0, 32, send_x, 0)
    opened(half_x, (x_send,))
    opened(half_x, (x_recv,))

    def add_block(h, o):
        part[...] += dot(xb[h * 4 + o], wb[h, o])

    part[...] = jnp.zeros_like(part)
    arrived(qv, (local, 1))
    arrived(gv, (local, 2))
    arrived(segv, (local, 3))
    across_lanes = jnp.broadcast_to(segv[...], (128, 128))
    same = across_lanes.T == across_lanes
    row = lax.broadcasted_iota(jnp.int32, (128, 128), 0)
    column = lax.broadcasted_iota(jnp.int32, (128, 128), 1)
    mask[...] = jnp.where(same & (row <= column), 0.0, -1e30)

    for d in (1, 3, 2):
        pass_on(0, d)
    heard(0)
    tell(1)
    for d in (0, 1, 3):
        relay(0, d)
    arrived(piece(1, outer, 0), (m_recv,))
    spread_inner(1, piece(1, outer, 0))
    spread_outer(1, 0, piece(1, outer, 0))
    relay(0, 2)
    heard(1)
    tell(2)
    arrived(first_w, (local, 0))
    arrived(half_x, (local, 4))
    arrived(half_x, (x_recv,))
    add_block(0, outer)
    add_block(0, left)
    add_block(0, right)
    for d in (1, 3):
        pass_on(1, d)
    relay(1, 0)
    pass_on(1, 2)
    for d in range(4):
        relayed(0, d)
    add_block(0, across)
    for d in (1, 3, 2):
        relay(1, d)
    add_block(1, outer)
    add_block(1, left)
    add_block(1, right)
    for d in range(4):
        relayed(1, d)
    add_block(1, across)

    send(part.at[pl.ds(128, 128), :], part_in, (c_send, 0), (c_recv, 0), partner)
    arrived(part_in, (c_recv, 0))
    keyval = (part[pl.ds(0, 128), :] + part_in[...]).astype(BF16)
    keys, values = keyval[:, :HEAD], keyval[:, HEAD:]

    d_keys = jnp.zeros((128, HEAD), F32)
    d_values = jnp.zeros((128, HEAD), F32)
    for n in range(QH):
        cols = pl.ds(n * HEAD, HEAD)
        q, g = qv[:, cols], gv[:, cols]
        scores = dot_nt(keys, q) * SCALE + mask[...]
        weights = jnp.exp(scores - jnp.max(scores, axis=0, keepdims=True))
        probs = weights * (1.0 / jnp.sum(weights, axis=0, keepdims=True))
        d_probs = dot_nt(values, g)
        low = probs.astype(BF16)
        delta = jnp.sum(low.astype(F32) * d_probs, axis=0, keepdims=True)
        d_score = (probs * (d_probs - delta)).astype(BF16)
        dst[:, cols] = d_score
        d_keys += dot(d_score, q)
        d_values += dot(low, g)
    dkv[pl.ds(0, 128), pl.ds(0, HEAD)] = (d_keys * SCALE).astype(BF16)
    dkv[pl.ds(0, 128), pl.ds(HEAD, HEAD)] = d_values.astype(BF16)
    send(dkv.at[pl.ds(0, 128), :], dkv.at[pl.ds(128, 128), :], (c_send, 1), (c_recv, 1), partner)

    for n in range(QH):
        cols = pl.ds(n * HEAD, HEAD)
        dq_ref[:, cols] = (dot_tn(dst[:, cols], keys) * SCALE).astype(BF16)
    arrived(dkv.at[pl.ds(128, 128), :], (c_recv, 1))

    heard(2)

    def term(h, o, d):
        return dot_tn(xb[((h + zh) % 2) * 4 + o, :, rows128((inner + d) % 4)], dkv[...])

    def send_far(h, d):
        far[h, d] = term(h, across, d).astype(BF16)
        send(far.at[h, d, pl.ds(0, 64), :], far_l.at[h, d], (r1_send, h, d, 0), (r1_recv, h, d, 0), on_outer(right))
        send(far.at[h, d, pl.ds(64, 64), :], far_r.at[h, d], (r1_send, h, d, 1), (r1_recv, h, d, 1), on_outer(left))

    def send_joined(h, d):
        to_right, to_left = term(h, right, d), term(h, left, d)
        arrived(far_l.at[h, d], (r1_recv, h, d, 0))
        joined[h, d, 0, pl.ds(0, 64), :] = (to_right[:64] + far_l[h, d].astype(F32)).astype(BF16)
        joined[h, d, 0, pl.ds(64, 64), :] = to_right[64:].astype(BF16)
        send(joined.at[h, d, 0], in_l.at[h, d], (r1_send, h, d, 2), (r1_recv, h, d, 2), on_outer(right))
        arrived(far_r.at[h, d], (r1_recv, h, d, 1))
        joined[h, d, 1, pl.ds(0, 64), :] = to_left[:64].astype(BF16)
        joined[h, d, 1, pl.ds(64, 64), :] = (to_left[64:] + far_r[h, d].astype(F32)).astype(BF16)
        send(joined.at[h, d, 1], in_r.at[h, d], (r1_send, h, d, 3), (r1_recv, h, d, 3), on_outer(left))

    def input_grad(h, o):
        k = h * 4 + o
        di[k] = dot_nt(dkv[...], wb[h, o]).astype(BF16)

    def store_dx(n, _):
        k, frm, to = x_columns(n, core)
        pltpu.make_async_copy(
            di.at[k, pl.ds(0, 128), frm], dx_ref.at[:, to], local.at[6 + n // 16]
        ).start()
        remote(
            di.at[k, pl.ds(128, 128), frm], dx_ref.at[:, to], dx_send.at[n // 16], dx_recv.at[n // 16], partner
        ).start()
        return 0

    def write_dx(h):
        lax.fori_loop(h * 16, h * 16 + 16, store_dx, 0)
        quarter = xb.at[pl.ds(0, 2)]
        for sem in ((local, 6 + h), (dx_send, h), (dx_recv, h)):
            opened(quarter, sem)

    def outer_sum(h, d):
        total = term(h, outer, d)
        arrived(in_l.at[h, d], (r1_recv, h, d, 2))
        total += in_l[h, d].astype(F32)
        arrived(in_r.at[h, d], (r1_recv, h, d, 3))
        return total + in_r[h, d].astype(F32)

    def inner_ring(h, d):
        inner_out[h, d - 1] = outer_sum(h, d).astype(BF16)
        send(inner_out.at[h, d - 1], inner_in.at[h, d - 1], (r2_send, h, d - 1),
             (r2_recv, h, d - 1), on_inner((inner + d) % 4))

    def plane_sum(h):
        total = outer_sum(h, 0)
        for d in (2, 1, 3):
            arrived(inner_in.at[h, d - 1], (r2_recv, h, d - 1))
            total += inner_in[h, d - 1].astype(F32)
        z_out[h] = total.astype(BF16)

        def each(act):
            for low in range(8):
                ahead = (8 * h + low - z + 16) % 16

                @pl.when(ahead != 0)
                def _():
                    act(remote(z_out.at[h, pl.ds(low * 16, 16), :], z_in.at[ahead],
                               z_send.at[h, low], z_recv.at[ahead], on_z(h, low)))

        each(lambda copy: copy.start())
        opened(lambda: each(lambda copy: copy.wait_send()), (z_send, h))

    order = [(h, d) for h in (0, 1) for d in (2, 1, 3, 0)]
    for h, d in order:
        send_far(h, d)
    for h, d in order:
        send_joined(h, d)
    for d in (2, 1, 3):
        inner_ring(0, d)
    inner_ring(1, 2)
    inner_ring(1, 1)
    plane_sum(0)
    inner_ring(1, 3)
    plane_sum(1)
    for n in range(8):
        input_grad(n // 4, n % 4)
        if n % 4 == 3:
            write_dx(n // 4)

    def owned(low, at_core):
        return pl.ds(pl.multiple_of(at_core * 128 + low * 16, 16), 16)

    mine = owned(zl, core)
    total = z_out[zh, pl.ds(pl.multiple_of(zl * 16, 16), 16), :].astype(F32)
    for ahead in range(1, 16):
        pltpu.make_async_copy(z_in.at[ahead], z_in.at[ahead], z_recv.at[ahead]).wait()
        total += z_in[ahead].astype(F32)
    fin[mine, :] = total.astype(BF16)
    for n in range(7):
        low = n + (n >= zl).astype(jnp.int32)
        for other in (0, 1):
            at_core = core * (1 - other) + (1 - core) * other
            remote(fin.at[mine, :], fin.at[mine, :], f_send.at[other, n], f_recv.at[other, zl],
                   (low * 2 + at_core, shard)).start()
            opened(fin.at[mine, :], (f_send, other, n))
    send(fin.at[mine, :], fin.at[mine, :], (c_send, 2), (c_recv, 2), partner)
    arrived(fin.at[owned(zl, 1 - core), :], (c_recv, 2))
    for other in (0, 1):
        at_core = core * (1 - other) + (1 - core) * other
        for d in range(1, 8):
            low = (zl + d) % 8
            pltpu.make_async_copy(
                fin.at[owned(low, at_core), :], fin.at[owned(low, at_core), :], f_recv.at[other, low]
            ).wait()
    dw_ref[...] = fin[...].astype(F32)

    finish()


def store_kernel(a, b, c, a_out, b_out, c_out, sems):
    copies = [
        pltpu.make_async_copy(src, to, sems.at[n])
        for n, (src, to) in enumerate(((a, a_out), (b, b_out), (c, c_out)))
    ]
    for copy in copies:
        copy.start()
    for copy in copies:
        copy.wait()


def body(layer_input, queries, d_out, segment_ids, kv_weight):
    dma = pltpu.SemaphoreType.DMA
    any_space = pl.BlockSpec(memory_space=pl.ANY)
    shapes = (
        jax.ShapeDtypeStruct((128, 8192), BF16),
        jax.ShapeDtypeStruct((128, 512), BF16),
        jax.ShapeDtypeStruct((256, 256), F32),
    )
    results = pl.pallas_call(
        kernel,
        out_shape=shapes,
        in_specs=[pl.BlockSpec(memory_space=pltpu.HBM)] * 5,
        out_specs=(any_space,) + (pl.BlockSpec(memory_space=pltpu.VMEM),) * 2,
        scratch_shapes=[
            pltpu.VMEM((8, 256, 512), BF16),
            pltpu.VMEM((2, 4, 512, 256), BF16),
            pltpu.VMEM((128, 512), BF16),
            pltpu.VMEM((128, 512), BF16),
            pltpu.VMEM((1, 128), jnp.int32),
            pltpu.VMEM((128, 128), F32),
            pltpu.VMEM((256, 256), F32),
            pltpu.VMEM((128, 256), F32),
            pltpu.VMEM((128, 512), BF16),
            pltpu.VMEM((256, 256), BF16),
            pltpu.VMEM((8, 256, 512), BF16),
            pltpu.VMEM((2, 4, 128, 256), BF16),
            pltpu.VMEM((2, 4, 2, 128, 256), BF16),
            pltpu.VMEM((2, 4, 64, 256), BF16),
            pltpu.VMEM((2, 4, 64, 256), BF16),
            pltpu.VMEM((2, 4, 128, 256), BF16),
            pltpu.VMEM((2, 4, 128, 256), BF16),
            pltpu.VMEM((2, 3, 128, 256), BF16),
            pltpu.VMEM((2, 3, 128, 256), BF16),
            pltpu.VMEM((2, 128, 256), BF16),
            pltpu.VMEM((16, 16, 256), BF16),
            pltpu.VMEM((256, 256), BF16),
            dma((9,)),
            dma(()),
            dma(()),
            dma((2, 3)),
            dma((2, 3)),
            dma((2, 4, 4)),
            dma((2, 4, 4)),
            dma((4,)),
            dma(()),
            dma((3,)),
            dma((3,)),
            dma((2,)),
            dma((2,)),
            dma((2, 4, 4)),
            dma((2, 4, 4)),
            dma((2, 3)),
            dma((2, 3)),
            dma((2, 8)),
            dma((16,)),
            dma((2, 7)),
            dma((2, 8)),
            pltpu.SemaphoreType.REGULAR((3,)),
        ],
        compiler_params=pltpu.CompilerParams(
            collective_id=0, has_side_effects=True, vmem_limit_bytes=40 * 1024 * 1024
        ),
    )(*[
        pltpu.with_memory_space_constraint(a, pltpu.HBM)
        for a in (layer_input, queries, d_out, segment_ids, kv_weight)
    ])
    return pl.pallas_call(
        store_kernel,
        out_shape=shapes,
        in_specs=[any_space] * 3,
        out_specs=(any_space,) * 3,
        scratch_shapes=[dma((3,))],
        compiler_params=pltpu.CompilerParams(vmem_limit_bytes=4 * 1024 * 1024),
    )(*results)


def solution(mesh):
    return jax.shard_map(
        body,
        mesh=mesh,
        in_specs=(
            P(("rep", "shard"), None),
            P(("rep", "shard"), None),
            P(("rep", "shard"), None),
            P(("rep", "shard"), None),
            P("shard", None),
        ),
        out_specs=(P(("rep", "shard"), None), P(("rep", "shard"), None), P("shard", None)),
        check_vma=False,
    )
```

```python
import jax
import jax.numpy as jnp
from jax import lax
from jax.experimental import pallas as pl
from jax.experimental.pallas import tpu as pltpu
from jax.sharding import PartitionSpec as P

HEAD = 128
QH = 4
SCALE = 1.0 / HEAD**0.5
BF16 = jnp.bfloat16
F32 = jnp.float32
MESH = pl.DeviceIdType.MESH


def dot(a, b):
    return jnp.dot(a, b, preferred_element_type=F32)


def dot_nt(a, b):
    return lax.dot_general(a, b, (((1,), (1,)), ((), ())), preferred_element_type=F32)


def dot_tn(a, b):
    return lax.dot_general(a, b, (((0,), (0,)), ((), ())), preferred_element_type=F32)


def shard_at(zh, outer, inner, core):
    y = outer * (1 - core) + inner * core
    x = inner * (1 - core) + outer * core
    return zh * 16 + y * 4 + x


def kernel(
    x_ref, q_ref, g_ref, seg_ref, w_ref,
    dx_ref, dq_ref, dw_ref,
    xb, wb, qv, gv, segv, mask, part, part_in, dst, dkv, di,
    far, joined, far_l, far_r, in_l, in_r,
    inner_out, inner_in, z_out, z_in, fin,
    local, x_send, x_recv, w_send, w_recv, p2_send, p2_recv, m_send, m_recv,
    c_send, c_recv, dx_send, dx_recv, r1_send, r1_recv, r2_send, r2_recv,
    z_send, z_recv, f_send, f_recv, known,
):
    rep, shard = lax.axis_index("rep"), lax.axis_index("shard")
    core, zl = rep % 2, rep // 2
    zh, y, x = shard // 16, (shard // 4) % 4, shard % 4
    z = zh * 8 + zl
    outer = y * (1 - core) + x * core
    inner = x * (1 - core) + y * core
    right, left, across = (outer + 1) % 4, (outer + 3) % 4, (outer + 2) % 4

    def on_outer(o):
        return (rep, shard_at(zh, o, inner, core))

    def on_inner(i):
        return (rep, shard_at(zh, outer, i, core))

    def on_z(half, low):
        return (low * 2 + core, shard_at(half, outer, inner, core))

    partner = (zl * 2 + 1 - core, shard)
    is_edge = (zl == 0) | (zl == 7)

    def on_z_at(d):
        there = (z + d + 16) % 16
        return on_z(there // 8, there % 8)


    def rows128(i):
        return pl.ds(pl.multiple_of(i * 128, 128), 128)

    def remote(src, dst_, ssem, rsem, device):
        return pltpu.make_async_remote_copy(
            src_ref=src, dst_ref=dst_, send_sem=ssem, recv_sem=rsem,
            device_id=device, device_id_type=MESH,
        )

    started = {}

    def sem_of(name):
        return name[0].at[name[1:]] if len(name) > 1 else name[0]

    def key_of(name):
        return (id(name[0]),) + name[1:]

    def finish():
        for ref, sem in list(started.values()):
            if callable(ref):
                ref()
                del started[key_of(sem)]
            else:
                arrived(ref, sem)

    def opened(ref, sem):
        started[key_of(sem)] = (ref, sem)

    def arrived(ref, sem):
        del started[key_of(sem)]
        pltpu.make_async_copy(ref, ref, sem_of(sem)).wait()

    def send(src, dst_, ssem, rsem, device):
        remote(src, dst_, sem_of(ssem), sem_of(rsem), device).start()
        opened(src, ssem)
        opened(dst_, rsem)

    def copy_here(src, dst_, sem):
        pltpu.make_async_copy(src, dst_, sem_of(sem)).start()
        opened(dst_, sem)

    barrier = pltpu.get_barrier_semaphore()
    friends = [partner, on_outer(right), on_outer(left)]
    friends += [on_inner((inner + d) % 4) for d in (1, 2, 3)]
    friends += [on_z_at(1), on_z_at(-1)]
    near = len(friends)
    friends.append(on_z(1 - zh, 7 * (1 - zl // 4)))
    for friend in friends:
        pl.semaphore_signal(barrier, inc=1, device_id=friend, device_id_type=MESH)

    own_w = w_ref.at[rows128(core), :]
    first_w = wb.at[0, outer, rows128(inner), :]
    copy_here(own_w, first_w, (local, 0))
    copy_here(q_ref, qv, (local, 1))
    copy_here(g_ref, gv, (local, 2))
    copy_here(seg_ref, segv, (local, 3))

    def x_columns(n, for_core):
        k, i = n // 4, n % 4
        half, o = (k // 4 + zh) % 2, k % 4
        column = shard_at(half, o, i, for_core) * 256 + for_core * 128
        return k, pl.ds(pl.multiple_of(i * 128, 128), 128), pl.ds(pl.multiple_of(column, 128), 128)

    def load_x(n, _):
        k, to, frm = x_columns(n, core)
        pltpu.make_async_copy(
            x_ref.at[:, frm], xb.at[k, pl.ds(0, 128), to], local.at[4]
        ).start()
        return 0

    half_x = xb.at[pl.ds(0, 4)]
    pl.semaphore_wait(barrier, near + 4 * is_edge.astype(jnp.int32))

    def tell(n):
        for d in (1 << n, -(1 << n)):
            pl.semaphore_signal(known.at[n], inc=1, device_id=on_z_at(d), device_id_type=MESH)

    def heard(n):
        pl.semaphore_wait(known.at[n], 2)


    def border(n):
        edge = zl // 7
        low = (3 - n) * edge + (4 + n) * (1 - edge)
        return remote(own_w, wb.at[1, outer, rows128(inner), :], m_send.at[n], m_recv, on_z(1 - zh, low))

    @pl.when(is_edge)
    def _():
        for n in range(4):
            border(n).start()

    def border_sent():
        @pl.when(is_edge)
        def _():
            for n in range(4):
                border(n).wait_send()

    opened(border_sent, (m_send,))
    opened(first_w, (m_recv,))

    def piece(h, o, d):
        return wb.at[h, o, rows128((inner - d + 4) % 4), :]

    def spread_inner(h, src):
        for d in (2, 1, 3):
            send(src, piece(h, outer, 0), (w_send, h, d - 1), (w_recv, h, d - 1), on_inner((inner + d) % 4))

    def spread_outer(h, d, src):
        to = piece(h, outer, d)
        send(src, to, (p2_send, h, d, 0), (p2_recv, h, d, 0), on_outer(right))
        send(src, to, (p2_send, h, d, 1), (p2_recv, h, d, 1), on_outer(left))

    def pass_on(h, d):
        arrived(piece(h, outer, d), (w_recv, h, d - 1))
        spread_outer(h, d, piece(h, outer, d))

    def relay(h, d):
        first = ((inner - d + 4) % 4) * 128
        arrived(piece(h, left, d), (p2_recv, h, d, 0))
        half = wb.at[h, left, pl.ds(pl.multiple_of(first, 128), 64), :]
        send(half, half, (p2_send, h, d, 2), (p2_recv, h, d, 2), on_outer(right))
        arrived(piece(h, right, d), (p2_recv, h, d, 1))
        half = wb.at[h, right, pl.ds(pl.multiple_of(first + 64, 64), 64), :]
        send(half, half, (p2_send, h, d, 3), (p2_recv, h, d, 3), on_outer(left))

    def relayed(h, d):
        first = ((inner - d + 4) % 4) * 128
        arrived(wb.at[h, across, pl.ds(pl.multiple_of(first, 128), 64), :], (p2_recv, h, d, 2))
        arrived(wb.at[h, across, pl.ds(pl.multiple_of(first + 64, 64), 64), :], (p2_recv, h, d, 3))

    spread_inner(0, own_w)
    spread_outer(0, 0, own_w)
    tell(0)

    def send_x(n, _):
        k, to, frm = x_columns(n, 1 - core)
        remote(
            x_ref.at[:, frm], xb.at[k, pl.ds(128, 128), to], x_send, x_recv, partner
        ).start()
        return 0

    lax.fori_loop(0, 32, load_x, 0)
    opened(half_x, (local, 4))
    lax.fori_loop(0, 32, send_x, 0)
    opened(half_x, (x_send,))
    opened(half_x, (x_recv,))

    def add_block(h, o):
        part[...] += dot(xb[h * 4 + o], wb[h, o])

    part[...] = jnp.zeros_like(part)
    arrived(qv, (local, 1))
    arrived(gv, (local, 2))
    arrived(segv, (local, 3))
    across_lanes = jnp.broadcast_to(segv[...], (128, 128))
    same = across_lanes.T == across_lanes
    row = lax.broadcasted_iota(jnp.int32, (128, 128), 0)
    column = lax.broadcasted_iota(jnp.int32, (128, 128), 1)
    mask[...] = jnp.where(same & (row <= column), 0.0, -1e30)

    for d in (1, 3, 2):
        pass_on(0, d)
    heard(0)
    tell(1)
    for d in (0, 1, 3):
        relay(0, d)
    arrived(piece(1, outer, 0), (m_recv,))
    spread_inner(1, piece(1, outer, 0))
    spread_outer(1, 0, piece(1, outer, 0))
    relay(0, 2)
    heard(1)
    tell(2)
    arrived(first_w, (local, 0))
    arrived(half_x, (local, 4))
    arrived(half_x, (x_recv,))
    add_block(0, outer)
    add_block(0, left)
    add_block(0, right)
    for d in (1, 3):
        pass_on(1, d)
    relay(1, 0)
    pass_on(1, 2)
    for d in range(4):
        relayed(0, d)
    add_block(0, across)
    for d in (1, 3, 2):
        relay(1, d)
    add_block(1, outer)
    add_block(1, left)
    add_block(1, right)
    for d in range(4):
        relayed(1, d)
    add_block(1, across)

    send(part.at[pl.ds(128, 128), :], part_in, (c_send, 0), (c_recv, 0), partner)
    arrived(part_in, (c_recv, 0))
    keyval = (part[pl.ds(0, 128), :] + part_in[...]).astype(BF16)
    keys, values = keyval[:, :HEAD], keyval[:, HEAD:]

    d_keys = jnp.zeros((128, HEAD), F32)
    d_values = jnp.zeros((128, HEAD), F32)
    for n in range(QH):
        cols = pl.ds(n * HEAD, HEAD)
        q, g = qv[:, cols], gv[:, cols]
        scores = dot_nt(keys, q) * SCALE + mask[...]
        weights = jnp.exp(scores - jnp.max(scores, axis=0, keepdims=True))
        probs = weights * (1.0 / jnp.sum(weights, axis=0, keepdims=True))
        d_probs = dot_nt(values, g)
        low = probs.astype(BF16)
        delta = jnp.sum(low.astype(F32) * d_probs, axis=0, keepdims=True)
        d_score = (probs * (d_probs - delta)).astype(BF16)
        dst[:, cols] = d_score
        d_keys += dot(d_score, q)
        d_values += dot(low, g)
    dkv[pl.ds(0, 128), pl.ds(0, HEAD)] = (d_keys * SCALE).astype(BF16)
    dkv[pl.ds(0, 128), pl.ds(HEAD, HEAD)] = d_values.astype(BF16)
    send(dkv.at[pl.ds(0, 128), :], dkv.at[pl.ds(128, 128), :], (c_send, 1), (c_recv, 1), partner)

    for n in range(QH):
        cols = pl.ds(n * HEAD, HEAD)
        dq_ref[:, cols] = (dot_tn(dst[:, cols], keys) * SCALE).astype(BF16)
    arrived(dkv.at[pl.ds(128, 128), :], (c_recv, 1))

    heard(2)

    def term(h, o, d):
        return dot_tn(xb[((h + zh) % 2) * 4 + o, :, rows128((inner + d) % 4)], dkv[...])

    def send_far(h, d):
        far[h, d] = term(h, across, d).astype(BF16)
        send(far.at[h, d, pl.ds(0, 64), :], far_l.at[h, d], (r1_send, h, d, 0), (r1_recv, h, d, 0), on_outer(right))
        send(far.at[h, d, pl.ds(64, 64), :], far_r.at[h, d], (r1_send, h, d, 1), (r1_recv, h, d, 1), on_outer(left))

    def send_joined(h, d):
        to_right, to_left = term(h, right, d), term(h, left, d)
        arrived(far_l.at[h, d], (r1_recv, h, d, 0))
        joined[h, d, 0, pl.ds(0, 64), :] = (to_right[:64] + far_l[h, d].astype(F32)).astype(BF16)
        joined[h, d, 0, pl.ds(64, 64), :] = to_right[64:].astype(BF16)
        send(joined.at[h, d, 0], in_l.at[h, d], (r1_send, h, d, 2), (r1_recv, h, d, 2), on_outer(right))
        arrived(far_r.at[h, d], (r1_recv, h, d, 1))
        joined[h, d, 1, pl.ds(0, 64), :] = to_left[:64].astype(BF16)
        joined[h, d, 1, pl.ds(64, 64), :] = (to_left[64:] + far_r[h, d].astype(F32)).astype(BF16)
        send(joined.at[h, d, 1], in_r.at[h, d], (r1_send, h, d, 3), (r1_recv, h, d, 3), on_outer(left))

    def input_grad(h, o):
        k = h * 4 + o
        di[k] = dot_nt(dkv[...], wb[h, o]).astype(BF16)

    def store_dx(n, _):
        k, frm, to = x_columns(n, core)
        pltpu.make_async_copy(
            di.at[k, pl.ds(0, 128), frm], dx_ref.at[:, to], local.at[6 + n // 16]
        ).start()
        remote(
            di.at[k, pl.ds(128, 128), frm], dx_ref.at[:, to], dx_send.at[n // 16], dx_recv.at[n // 16], partner
        ).start()
        return 0

    def write_dx(h):
        lax.fori_loop(h * 16, h * 16 + 16, store_dx, 0)
        quarter = xb.at[pl.ds(0, 2)]
        for sem in ((local, 6 + h), (dx_send, h), (dx_recv, h)):
            opened(quarter, sem)

    def outer_sum(h, d):
        total = term(h, outer, d)
        arrived(in_l.at[h, d], (r1_recv, h, d, 2))
        total += in_l[h, d].astype(F32)
        arrived(in_r.at[h, d], (r1_recv, h, d, 3))
        return total + in_r[h, d].astype(F32)

    def inner_ring(h, d):
        inner_out[h, d - 1] = outer_sum(h, d).astype(BF16)
        send(inner_out.at[h, d - 1], inner_in.at[h, d - 1], (r2_send, h, d - 1),
             (r2_recv, h, d - 1), on_inner((inner + d) % 4))

    def plane_sum(h):
        total = outer_sum(h, 0)
        for d in (2, 1, 3):
            arrived(inner_in.at[h, d - 1], (r2_recv, h, d - 1))
            total += inner_in[h, d - 1].astype(F32)
        z_out[h] = total.astype(BF16)

        def each(act):
            for low in range(8):
                ahead = (8 * h + low - z + 16) % 16

                @pl.when(ahead != 0)
                def _():
                    act(remote(z_out.at[h, pl.ds(low * 16, 16), :], z_in.at[ahead],
                               z_send.at[h, low], z_recv.at[ahead], on_z(h, low)))

        each(lambda copy: copy.start())
        opened(lambda: each(lambda copy: copy.wait_send()), (z_send, h))

    order = [(h, d) for h in (0, 1) for d in (2, 1, 3, 0)]
    for h, d in order:
        send_far(h, d)
    for h, d in order:
        send_joined(h, d)
    for d in (2, 1, 3):
        inner_ring(0, d)
    inner_ring(1, 2)
    inner_ring(1, 1)
    plane_sum(0)
    inner_ring(1, 3)
    plane_sum(1)
    for n in range(4):
        input_grad(0, n)
    write_dx(0)

    def owned(low, at_core):
        return pl.ds(pl.multiple_of(at_core * 128 + low * 16, 16), 16)

    mine = owned(zl, core)
    total = z_out[zh, pl.ds(pl.multiple_of(zl * 16, 16), 16), :].astype(F32)
    for ahead in range(1, 16):
        pltpu.make_async_copy(z_in.at[ahead], z_in.at[ahead], z_recv.at[ahead]).wait()
        total += z_in[ahead].astype(F32)
    fin[mine, :] = total.astype(BF16)
    for n in range(7):
        low = n + (n >= zl).astype(jnp.int32)
        for other in (0, 1):
            at_core = core * (1 - other) + (1 - core) * other
            remote(fin.at[mine, :], fin.at[mine, :], f_send.at[other, n], f_recv.at[other, zl],
                   (low * 2 + at_core, shard)).start()
            opened(fin.at[mine, :], (f_send, other, n))
    send(fin.at[mine, :], fin.at[mine, :], (c_send, 2), (c_recv, 2), partner)
    for n in range(4):
        input_grad(1, n)
    write_dx(1)
    arrived(fin.at[owned(zl, 1 - core), :], (c_recv, 2))
    for other in (0, 1):
        at_core = core * (1 - other) + (1 - core) * other
        for d in range(1, 8):
            low = (zl + d) % 8
            pltpu.make_async_copy(
                fin.at[owned(low, at_core), :], fin.at[owned(low, at_core), :], f_recv.at[other, low]
            ).wait()
    dw_ref[...] = fin[...].astype(F32)

    finish()


def store_kernel(a, b, c, a_out, b_out, c_out, sems):
    copies = [
        pltpu.make_async_copy(src, to, sems.at[n])
        for n, (src, to) in enumerate(((a, a_out), (b, b_out), (c, c_out)))
    ]
    for copy in copies:
        copy.start()
    for copy in copies:
        copy.wait()


def body(layer_input, queries, d_out, segment_ids, kv_weight):
    dma = pltpu.SemaphoreType.DMA
    any_space = pl.BlockSpec(memory_space=pl.ANY)
    shapes = (
        jax.ShapeDtypeStruct((128, 8192), BF16),
        jax.ShapeDtypeStruct((128, 512), BF16),
        jax.ShapeDtypeStruct((256, 256), F32),
    )
    results = pl.pallas_call(
        kernel,
        out_shape=shapes,
        in_specs=[pl.BlockSpec(memory_space=pltpu.HBM)] * 5,
        out_specs=(any_space,) + (pl.BlockSpec(memory_space=pltpu.VMEM),) * 2,
        scratch_shapes=[
            pltpu.VMEM((8, 256, 512), BF16),
            pltpu.VMEM((2, 4, 512, 256), BF16),
            pltpu.VMEM((128, 512), BF16),
            pltpu.VMEM((128, 512), BF16),
            pltpu.VMEM((1, 128), jnp.int32),
            pltpu.VMEM((128, 128), F32),
            pltpu.VMEM((256, 256), F32),
            pltpu.VMEM((128, 256), F32),
            pltpu.VMEM((128, 512), BF16),
            pltpu.VMEM((256, 256), BF16),
            pltpu.VMEM((8, 256, 512), BF16),
            pltpu.VMEM((2, 4, 128, 256), BF16),
            pltpu.VMEM((2, 4, 2, 128, 256), BF16),
            pltpu.VMEM((2, 4, 64, 256), BF16),
            pltpu.VMEM((2, 4, 64, 256), BF16),
            pltpu.VMEM((2, 4, 128, 256), BF16),
            pltpu.VMEM((2, 4, 128, 256), BF16),
            pltpu.VMEM((2, 3, 128, 256), BF16),
            pltpu.VMEM((2, 3, 128, 256), BF16),
            pltpu.VMEM((2, 128, 256), BF16),
            pltpu.VMEM((16, 16, 256), BF16),
            pltpu.VMEM((256, 256), BF16),
            dma((9,)),
            dma(()),
            dma(()),
            dma((2, 3)),
            dma((2, 3)),
            dma((2, 4, 4)),
            dma((2, 4, 4)),
            dma((4,)),
            dma(()),
            dma((3,)),
            dma((3,)),
            dma((2,)),
            dma((2,)),
            dma((2, 4, 4)),
            dma((2, 4, 4)),
            dma((2, 3)),
            dma((2, 3)),
            dma((2, 8)),
            dma((16,)),
            dma((2, 7)),
            dma((2, 8)),
            pltpu.SemaphoreType.REGULAR((3,)),
        ],
        compiler_params=pltpu.CompilerParams(
            collective_id=0, has_side_effects=True, vmem_limit_bytes=40 * 1024 * 1024
        ),
    )(*[
        pltpu.with_memory_space_constraint(a, pltpu.HBM)
        for a in (layer_input, queries, d_out, segment_ids, kv_weight)
    ])
    return pl.pallas_call(
        store_kernel,
        out_shape=shapes,
        in_specs=[any_space] * 3,
        out_specs=(any_space,) * 3,
        scratch_shapes=[dma((3,))],
        compiler_params=pltpu.CompilerParams(vmem_limit_bytes=4 * 1024 * 1024),
    )(*results)


def solution(mesh):
    return jax.shard_map(
        body,
        mesh=mesh,
        in_specs=(
            P(("rep", "shard"), None),
            P(("rep", "shard"), None),
            P(("rep", "shard"), None),
            P(("rep", "shard"), None),
            P("shard", None),
        ),
        out_specs=(P(("rep", "shard"), None), P(("rep", "shard"), None), P("shard", None)),
        check_vma=False,
    )
```
